32 devices in a mesh: dp: 4 (over y, x), shard: 8 (over z, core).
Axes of the slice: x: 2, y: 2, z: 4, core: 2. Of those that a mesh axis runs over, the one named last changes fastest.
Arguments:
- grads: float32 [4, 1, 2, 4096, 4096], P('dp', None, None, None, 'shard'), may hold values from -6 to 6
- params: float32 [1, 2, 4096, 4096], P(None, None, ('dp', 'shard')), may hold values from -0.09375 to 0.09375
- moment_one: float32 [1, 2, 4096, 4096], P(None, None, ('dp', 'shard')), may hold values from -0.75 to 0.75
- moment_two: float32 [1, 2, 4096, 4096], P(None, None, ('dp', 'shard')), may hold values from 1e-05 to 0.01
- relation_ids: int32 [1], replicated, may hold values from 0 to 63
- rates: float32 [64], replicated, may hold values from 0.02 to 0.1
- step_count: int32 [1], replicated, may hold values from 1 to 8
Outputs:
- new_params: float32 [1, 2, 4096, 4096], P(None, None, ('dp', 'shard'))
- new_moment_one: float32 [1, 2, 4096, 4096], P(None, None, ('dp', 'shard'))
- new_moment_two: float32 [1, 2, 4096, 4096], P(None, None, ('dp', 'shard'))
- panels: bfloat16 [1, 2, 4096, 4096], P(None, None, None, 'shard')
The draws below stay inside these ranges and needn't reach their ends.
Inputs may be any that keep to these rules, and one draw needn't show every extreme that they name: `relation_ids`: relation ids are edge types. `step_count`: the step count is positive.
All inputs are finite; a program needn't handle non-finite values.
Results may differ from the reference program's by a relative error of at most 0.001.
Values may be sent and summed in bfloat16 or wider, within the bound.
A program may use at most 128 MiB of HBM per device.

```python
import math
import jax
import jax.numpy as jnp
from jax import lax

D = 4096
NTYPES = 64
RW = 1
N_DP = 4


def block_scale(own_key, extent, shards, low, largest):
    def one(dim, shards_of):
        draws = jax.random.uniform(jax.random.fold_in(jax.random.fold_in(own_key, 6), dim), (shards_of,), jnp.float32, low / len(shards), largest / len(shards))
        return jnp.repeat(jnp.exp(draws), extent[dim] // shards_of).reshape((-1,) + (1,) * (len(extent) - dim - 1))

    level = one(*shards[0])
    for cut in shards[1:]:
        level = level * one(*cut)
    return level


def bell_draw(own_key, shape, width, most, shards=(), kind=jnp.bfloat16):
    result = width * jax.random.normal(own_key, shape, jnp.float32)
    if shards:
        result = result * block_scale(own_key, shape, shards, -0.22, 0.18)
    return jnp.clip(result, -most, most).astype(kind)


def setup_inputs(seed: int = 0) -> dict:
    streams_of = jax.random.split(jax.random.key(seed), 8)
    return {
        "grads": bell_draw(streams_of[0], (N_DP, RW, 2, D, D), 1.0, 6.0, ((0, 4), (4, 8)), jnp.float32),
        "params": bell_draw(streams_of[1], (RW, 2, D, D), D ** -0.5, 0.09375, ((2, 32),), jnp.float32),
        "moment_one": bell_draw(streams_of[2], (RW, 2, D, D), 0.05, 0.75, ((2, 32),), jnp.float32),
        "moment_two": jnp.clip(jnp.exp(math.log(0.01) - 6.9077553 * jax.random.uniform(streams_of[3], (RW, 2, D, D), jnp.float32) ** block_scale(streams_of[3], (RW, 2, D, D), ((2, 32),), -0.2, 0.2)), 9.999999747378752e-06, 0.01),
        "relation_ids": jax.random.randint(streams_of[4], (RW,), 0, NTYPES).astype(jnp.int32),
        "rates": jnp.clip(jnp.exp(jax.random.uniform(streams_of[5], (NTYPES,), jnp.float32, math.log(0.02), math.log(0.1))), 0.02, 0.1),
        "step_count": jax.random.randint(streams_of[6], (1,), 1, 9).astype(jnp.int32),
    }


def reference(grads, params, moment_one, moment_two, relation_ids, rates, step_count):
    gradient = lax.optimization_barrier(jnp.sum(grads, axis=0)) / N_DP
    onehot = (relation_ids[:, None] == jnp.arange(rates.shape[0], dtype=jnp.int32)[None, :]).astype(jnp.float32)
    learn = lax.optimization_barrier(jnp.sum(onehot * rates[None, :], axis=1))[:, None, None, None]
    new_one = 0.9 * moment_one + 0.1 * gradient
    new_two = 0.95 * moment_two + 0.05 * gradient * gradient
    steps = step_count[0].astype(jnp.float32)
    fix_one = 1.0 - jnp.power(jnp.float32(0.9), steps)
    fix_two = 1.0 - jnp.power(jnp.float32(0.95), steps)
    update = new_one / fix_one / (jnp.sqrt(new_two / fix_two) + 1e-08) + 0.1 * params
    new_params = params - learn * update
    return (new_params, new_one, new_two, new_params.astype(jnp.bfloat16))
```

```python
import functools
import math

import jax
import jax.numpy as jnp
from jax import lax
from jax.experimental import pallas as pl
from jax.experimental.pallas import tpu as pltpu
from jax.sharding import PartitionSpec as P

LIMIT = 6.0
TOP = 32700.0
MESH = pl.DeviceIdType.MESH
LAGS = (0, 2, 3, 4, 5, 6)
ROWS = 32


def encode(x, limit):
    root = x * lax.rsqrt(jnp.abs(x) + 1e-30) * (TOP / math.sqrt(limit))
    return jnp.round(root).astype(jnp.int32).astype(jnp.int16)


def decode(code, limit):
    root = code.astype(jnp.int32).astype(jnp.float32)
    return root * jnp.abs(root) * (limit / TOP**2)


def kernel(sizes, scal, grads, params, mone, mtwo, o_p, o_1, o_2, panels,
           gb, vp, v1, v2, c1, r1, c2, r2, r3, pan,
           g_sem, in_sem, out_sem, own_sem, s1s, s1r, s2s, s2r, s3s, s3r, s4s, s4r, s5s, s5r, s6s, s6r):
    na, nb, n_sh, mats, relations, rows, splits, pc = sizes
    n_dp = na * nb
    chunks = mats * splits
    dpi = lax.axis_index("dp")
    me = lax.axis_index("shard")
    a, b = dpi // nb, dpi % nb

    def geometry(k):
        m, c = k // splits, k % splits
        return m, pl.ds(c * rows, rows)

    def dims(k):
        if k % 2 == 0:
            return na, nb, a, b, lambda f, g: f * nb + g
        return nb, na, b, a, lambda f, g: g * nb + f

    def load(k):
        m, r = geometry(k)
        nf, ng = dims(k)[:2]
        for f in range(nf):
            if k % 2 == 0:
                src = grads.at[m, f, :, :, r, :]
            else:
                src = grads.at[m, :, f, :, r, :]
            pltpu.make_async_copy(src, gb.at[k, pl.ds(f * ng, ng)], g_sem.at[k]).start()
        for i, (src, dst) in enumerate(((params, vp), (mone, v1), (mtwo, v2))):
            pltpu.make_async_copy(src.at[m, r, :], dst.at[k], in_sem.at[i, k]).start()

    def remote(src, dst, ss, rs, dp, sh):
        return pltpu.make_async_remote_copy(
            src_ref=src, dst_ref=dst, send_sem=ss, recv_sem=rs,
            device_id=(dp, sh), device_id_type=MESH)

    def one(k, j):
        nf, ng, f, g, flat = dims(k)
        part = pl.ds((j - 1) * ng, ng)
        return remote(c1.at[k, part], r1.at[k, part], s1s.at[k, j - 1], s1r.at[k, j - 1],
                      flat((f + j) % nf, g), me)

    def two(k, j):
        nf, ng, f, g, flat = dims(k)
        return remote(c2.at[k, j - 1], r2.at[k, j - 1], s2s.at[k, j - 1], s2r.at[k, j - 1],
                      flat(f, (g + j) % ng), me)

    def stage0(k):
        nf, ng, f, g, flat = dims(k)
        pltpu.make_async_copy(gb.at[k], gb.at[k], g_sem.at[k]).wait()
        for j in range(1, nf):
            to = (f + j) % nf

            def body(i, _):
                for h in range(ng):
                    c1[k, (j - 1) * ng + h, i] = encode(gb[k, to * ng + h, i], LIMIT)
                return 0

            lax.fori_loop(0, n_sh, body, 0)
            one(k, j).start()

    def stage1(k):
        nf, ng, f, g, flat = dims(k)
        for j in range(1, nf):
            one(k, j).wait_recv()

        def total(h, i):
            value = gb[k, f * ng + h, i]
            for j in range(1, nf):
                value = value + decode(r1[k, (j - 1) * ng + h, i], LIMIT)
            return value

        for j in range(1, ng):
            to = (g + j) % ng

            def body(i, _):
                c2[k, j - 1, i] = encode(total(to, i), LIMIT * nf)
                return 0

            lax.fori_loop(0, n_sh, body, 0)
            two(k, j).start()

        def own(i, _):
            gb[k, f * ng + g, i] = total(g, i)
            return 0

        lax.fori_loop(0, n_sh, own, 0)

    def stage2(k):
        nf, ng, f, g, flat = dims(k)
        for j in range(1, ng):
            two(k, j).wait_recv()

        def body(i, _):
            value = gb[k, f * ng + g, i]
            for j in range(1, ng):
                value = value + decode(r2[k, j - 1, i], LIMIT * nf)
            gb[k, f * ng + g, i] = value
            return 0

        lax.fori_loop(0, n_sh, body, 0)

        def send(j, _):
            to = (me + j) % n_sh
            remote(gb.at[k, f * ng + g, to], r3.at[k, j - 1], s3s.at[k], s3r.at[k], dpi, to).start()
            return 0

        lax.fori_loop(1, n_sh, send, 0)

    def stage3(k):
        m, r = geometry(k)
        nf, ng, f, g, flat = dims(k)
        some = r3.at[k]
        pltpu.make_async_copy(some, some, s3r.at[k]).wait()
        for i, dst in enumerate((vp, v1, v2)):
            pltpu.make_async_copy(dst.at[k], dst.at[k], in_sem.at[i, k]).wait()
        rel = m // (mats // relations)
        learn = scal[2 + rel]
        inv_one, inv_two = scal[0], scal[1]

        def update(total, s):
            cols = pl.ds(pl.multiple_of(s * pc, 128), pc)
            gradient = total * (1.0 / n_dp)
            p = vp[k, :, cols]
            new_one = 0.9 * v1[k, :, cols] + 0.1 * gradient
            new_two = 0.95 * v2[k, :, cols] + 0.05 * gradient * gradient
            step = (new_one * inv_one) / (jnp.sqrt(new_two * inv_two) + 1e-08) + 0.1 * p
            new_p = p - learn * step
            vp[k, :, cols] = new_p
            v1[k, :, cols] = new_one
            v2[k, :, cols] = new_two
            pan[k, s] = new_p.astype(jnp.bfloat16)

        def body(j, _):
            s = (me + n_sh - j) % n_sh
            update(r3[k, j - 1], s)
            remote(pan.at[k, s], panels.at[m, a, b, me, r, :], s4s.at[k], s4r.at[k], dpi, s).start()
            return 0

        lax.fori_loop(1, n_sh, body, 0)
        update(gb[k, f * ng + g, me], me)
        pltpu.make_async_copy(pan.at[k, me], panels.at[m, a, b, me, r, :], own_sem.at[k]).start()
        for i, (src, dst) in enumerate(((vp, o_p), (v1, o_1), (v2, o_2))):
            pltpu.make_async_copy(src.at[k], dst.at[m, r, :], out_sem.at[i, k]).start()

    def five(k, j, came=False):
        m, r = geometry(k)
        nf, ng, f, g, flat = dims(k)
        block = panels.at[m, a, b, :, r, :]
        return remote(block, block, s5s.at[k, j - 1], s5r.at[k, j - 1], flat((f + j) % nf, g), me)

    def stage4(k):
        m, r = geometry(k)
        nf = dims(k)[0]
        some = panels.at[m, a, b, pl.ds(0, n_sh - 1), r, :]
        pltpu.make_async_copy(some, some, s4r.at[k]).wait()
        pltpu.make_async_copy(pan.at[k, me], panels.at[m, a, b, me, r, :], own_sem.at[k]).wait()
        for j in range(1, nf):
            five(k, j).start()

    def six(k, j):
        m, r = geometry(k)
        nf, ng, f, g, flat = dims(k)
        block = panels.at[m, :, b, :, r, :] if k % 2 == 0 else panels.at[m, a, :, :, r, :]
        return remote(block, block, s6s.at[k, j - 1], s6r.at[k, j - 1], flat(f, (g + j) % ng), me)

    def stage5(k):
        nf, ng = dims(k)[:2]
        for j in range(1, nf):
            five(k, j).wait_recv()
        for j in range(1, ng):
            six(k, j).start()

    for k in range(chunks):
        load(k)

    barrier = pltpu.get_barrier_semaphore()
    for j in range(1, na):
        pl.semaphore_signal(barrier, inc=1, device_id=(((a + j) % na) * nb + b, me), device_id_type=MESH)
    for j in range(1, nb):
        pl.semaphore_signal(barrier, inc=1, device_id=(a * nb + (b + j) % nb, me), device_id_type=MESH)
    for j in range(1, n_sh):
        pl.semaphore_signal(barrier, inc=1, device_id=(dpi, (me + j) % n_sh), device_id_type=MESH)
    pl.semaphore_wait(barrier, na - 1 + nb - 1 + n_sh - 1)

    stages = (stage0, stage1, stage2, stage3, stage4, stage5)
    for t in range(chunks + LAGS[-1]):
        for n in (0, 5, 4, 3, 2, 1):
            k = t - LAGS[n]
            if 0 <= k < chunks:
                stages[n](k)

    for k in range(chunks):
        m, r = geometry(k)
        nf, ng = dims(k)[:2]
        for j in range(1, nf):
            one(k, j).wait_send()
            five(k, j).wait_send()
        for j in range(1, ng):
            two(k, j).wait_send()
            six(k, j).wait_send()
            six(k, j).wait_recv()
        some = r3.at[k]
        pltpu.make_async_copy(some, some, s3s.at[k]).wait()
        some = pan.at[k, pl.ds(0, n_sh - 1)]
        pltpu.make_async_copy(some, some, s4s.at[k]).wait()
        for i, (src, dst) in enumerate(((vp, o_p), (v1, o_1), (v2, o_2))):
            pltpu.make_async_copy(src.at[k], dst.at[m, r, :], out_sem.at[i, k]).wait()


def body(grads, params, moment_one, moment_two, relation_ids, rates, step_count):
    n_dp = lax.axis_size("dp")
    n_sh = lax.axis_size("shard")
    relations = grads.shape[1]
    mats = relations * 2
    pc = grads.shape[-1]
    width = pc * n_sh
    owned = params.shape[2]
    nb = 2 if n_dp % 2 == 0 else 1
    na = n_dp // nb
    rows = min(ROWS, owned)
    splits = owned // rows
    chunks = mats * splits
    onehot = (relation_ids[:, None] == jnp.arange(rates.shape[0], dtype=jnp.int32)[None, :]).astype(
        jnp.float32
    )
    learn = jnp.sum(onehot * rates[None, :], axis=1)
    steps = step_count[0].astype(jnp.float32)
    fix_one = 1.0 - jnp.power(jnp.float32(0.9), steps)
    fix_two = 1.0 - jnp.power(jnp.float32(0.95), steps)
    scal = jnp.concatenate([jnp.stack([1.0 / fix_one, 1.0 / fix_two]), learn])
    pieces = grads.reshape(mats, na, nb, n_sh, owned, pc)
    flat = [x.reshape(mats, owned, width) for x in (params, moment_one, moment_two)]
    state = jax.ShapeDtypeStruct((mats, owned, width), jnp.float32)
    first = n_dp - min(na, nb)
    second = max(na, nb) - 1
    hand = pl.BlockSpec(memory_space=pl.ANY)
    dma = pltpu.SemaphoreType.DMA
    most = second
    out = pl.pallas_call(
        functools.partial(kernel, (na, nb, n_sh, mats, relations, rows, splits, pc)),
        out_shape=(state, state, state,
                   jax.ShapeDtypeStruct((mats, na, nb, n_sh, owned, pc), jnp.bfloat16)),
        in_specs=[pl.BlockSpec(memory_space=pltpu.SMEM)] + [hand] * 4,
        out_specs=(hand,) * 4,
        scratch_shapes=[
            pltpu.VMEM((chunks, n_dp, n_sh, rows, pc), jnp.float32),
            pltpu.VMEM((chunks, rows, width), jnp.float32),
            pltpu.VMEM((chunks, rows, width), jnp.float32),
            pltpu.VMEM((chunks, rows, width), jnp.float32),
            pltpu.VMEM((chunks, first, n_sh, rows, pc), jnp.int16),
            pltpu.VMEM((chunks, first, n_sh, rows, pc), jnp.int16),
            pltpu.VMEM((chunks, second, n_sh, rows, pc), jnp.int16),
            pltpu.VMEM((chunks, second, n_sh, rows, pc), jnp.int16),
            pltpu.VMEM((chunks, n_sh - 1, rows, pc), jnp.float32),
            pltpu.VMEM((chunks, n_sh, rows, pc), jnp.bfloat16),
            dma((chunks,)),
            dma((3, chunks)),
            dma((3, chunks)),
            dma((chunks,)),
            dma((chunks, most)), dma((chunks, most)),
            dma((chunks, most)), dma((chunks, most)),
            dma((chunks,)), dma((chunks,)),
            dma((chunks,)), dma((chunks,)),
            dma((chunks, most)), dma((chunks, most)),
            dma((chunks, most)), dma((chunks, most)),
        ],
        compiler_params=pltpu.CompilerParams(
            collective_id=0, has_side_effects=True, vmem_limit_bytes=56 * 1024 * 1024),
        cost_estimate=pl.CostEstimate(flops=50 * mats * owned * width, bytes_accessed=56 * mats * owned * width // 1,
                                      transcendentals=0),
    )(scal, pieces, *flat)
    new_params, new_one, new_two = (x.reshape(params.shape) for x in out[:3])
    panels = out[3].reshape(relations, 2, owned * n_sh * n_dp, pc)
    return (new_params, new_one, new_two, panels)


def solution(mesh):
    in_specs = (
        P("dp", None, None, None, "shard"),
        P(None, None, ("dp", "shard"), None),
        P(None, None, ("dp", "shard"), None),
        P(None, None, ("dp", "shard"), None),
        P(),
        P(),
        P(),
    )
    out_specs = (
        P(None, None, ("dp", "shard"), None),
        P(None, None, ("dp", "shard"), None),
        P(None, None, ("dp", "shard"), None),
        P(None, None, None, "shard"),
    )
    return jax.shard_map(body, mesh=mesh, in_specs=in_specs, out_specs=out_specs, check_vma=False)
```

```python
import functools
import math

import jax
import jax.numpy as jnp
from jax import lax
from jax.experimental import pallas as pl
from jax.experimental.pallas import tpu as pltpu
from jax.sharding import PartitionSpec as P

LIMIT = 6.0
TOP = 32700.0
SOFT = 0.61
MESH = pl.DeviceIdType.MESH
LAGS = (0, 2, 4, 6, 8, 10)
ROWS = 16


def encode(x, limit):
    soft = SOFT * math.sqrt(limit)
    scale = TOP * math.sqrt(limit**2 + soft**2) / limit
    bent = x * lax.rsqrt(x * x + soft**2) * scale
    return jnp.round(bent).astype(jnp.int32).astype(jnp.int16)


def decode(code, limit):
    soft = SOFT * math.sqrt(limit)
    scale = TOP * math.sqrt(limit**2 + soft**2) / limit
    bent = code.astype(jnp.int32).astype(jnp.float32) * (1.0 / scale)
    return bent * lax.rsqrt(1.0 - bent * bent) * soft


def kernel(sizes, scal, grads, params, mone, mtwo, o_p, o_1, o_2, panels,
           gb, vp, v1, v2, c1, r1, c2, r2, r3, pan,
           g_sem, in_sem, out_sem, own_sem, s1s, s1r, s2s, s2r, s3s, s3r, s4s, s4r, s5s, s5r, s6s, s6r):
    na, nb, n_sh, mats, relations, rows, splits, pc = sizes
    n_dp = na * nb
    chunks = mats * splits
    dpi = lax.axis_index("dp")
    me = lax.axis_index("shard")
    a, b = dpi // nb, dpi % nb

    def geometry(k):
        m, c = k // splits, k % splits
        return m, pl.ds(c * rows, rows)

    def dims(k):
        if k % 2 == 0:
            return na, nb, a, b, lambda f, g: f * nb + g
        return nb, na, b, a, lambda f, g: g * nb + f

    def load(k):
        m, r = geometry(k)
        nf, ng = dims(k)[:2]
        for f in range(nf):
            if k % 2 == 0:
                src = grads.at[m, f, :, :, r, :]
            else:
                src = grads.at[m, :, f, :, r, :]
            pltpu.make_async_copy(src, gb.at[k, pl.ds(f * ng, ng)], g_sem.at[k]).start()
        for i, (src, dst) in enumerate(((params, vp), (mone, v1), (mtwo, v2))):
            pltpu.make_async_copy(src.at[m, r, :], dst.at[k], in_sem.at[i, k]).start()

    def remote(src, dst, ss, rs, dp, sh):
        return pltpu.make_async_remote_copy(
            src_ref=src, dst_ref=dst, send_sem=ss, recv_sem=rs,
            device_id=(dp, sh), device_id_type=MESH)

    def one(k, j):
        nf, ng, f, g, flat = dims(k)
        part = pl.ds((j - 1) * ng, ng)
        return remote(c1.at[k, part], r1.at[k, part], s1s.at[k, j - 1], s1r.at[k, j - 1],
                      flat((f + j) % nf, g), me)

    def two(k, j):
        nf, ng, f, g, flat = dims(k)
        return remote(c2.at[k, j - 1], r2.at[k, j - 1], s2s.at[k, j - 1], s2r.at[k, j - 1],
                      flat(f, (g + j) % ng), me)

    def stage0(k):
        nf, ng, f, g, flat = dims(k)
        pltpu.make_async_copy(gb.at[k], gb.at[k], g_sem.at[k]).wait()
        for j in range(1, nf):
            to = (f + j) % nf

            def body(i, _):
                for h in range(ng):
                    c1[k, (j - 1) * ng + h, i] = encode(gb[k, to * ng + h, i], LIMIT)
                return 0

            lax.fori_loop(0, n_sh, body, 0)
            one(k, j).start()

    def stage1(k):
        nf, ng, f, g, flat = dims(k)
        for j in range(1, nf):
            one(k, j).wait_recv()

        def total(h, i):
            value = gb[k, f * ng + h, i]
            for j in range(1, nf):
                value = value + decode(r1[k, (j - 1) * ng + h, i], LIMIT)
            return value

        for j in range(1, ng):
            to = (g + j) % ng

            def body(i, _):
                c2[k, j - 1, i] = encode(total(to, i), LIMIT * nf)
                return 0

            lax.fori_loop(0, n_sh, body, 0)
            two(k, j).start()

        def own(i, _):
            gb[k, f * ng + g, i] = total(g, i)
            return 0

        lax.fori_loop(0, n_sh, own, 0)

    def stage2(k):
        nf, ng, f, g, flat = dims(k)
        for j in range(1, ng):
            two(k, j).wait_recv()

        def body(i, _):
            value = gb[k, f * ng + g, i]
            for j in range(1, ng):
                value = value + decode(r2[k, j - 1, i], LIMIT * nf)
            gb[k, f * ng + g, i] = value
            return 0

        lax.fori_loop(0, n_sh, body, 0)

        def send(j, _):
            to = (me + j) % n_sh
            remote(gb.at[k, f * ng + g, to], r3.at[k, j - 1], s3s.at[k], s3r.at[k], dpi, to).start()
            return 0

        lax.fori_loop(1, n_sh, send, 0)

    def stage3(k):
        m, r = geometry(k)
        nf, ng, f, g, flat = dims(k)
        some = r3.at[k]
        pltpu.make_async_copy(some, some, s3r.at[k]).wait()
        for i, dst in enumerate((vp, v1, v2)):
            pltpu.make_async_copy(dst.at[k], dst.at[k], in_sem.at[i, k]).wait()
        rel = m // (mats // relations)
        learn = scal[2 + rel]
        inv_one, inv_two = scal[0], scal[1]

        def update(total, s):
            cols = pl.ds(pl.multiple_of(s * pc, 128), pc)
            gradient = total * (1.0 / n_dp)
            p = vp[k, :, cols]
            new_one = 0.9 * v1[k, :, cols] + 0.1 * gradient
            new_two = 0.95 * v2[k, :, cols] + 0.05 * gradient * gradient
            step = (new_one * inv_one) / (jnp.sqrt(new_two * inv_two) + 1e-08) + 0.1 * p
            new_p = p - learn * step
            vp[k, :, cols] = new_p
            v1[k, :, cols] = new_one
            v2[k, :, cols] = new_two
            pan[k, s] = new_p.astype(jnp.bfloat16)

        def body(j, _):
            s = (me + n_sh - j) % n_sh
            update(r3[k, j - 1], s)
            remote(pan.at[k, s], panels.at[m, a, b, me, r, :], s4s.at[k], s4r.at[k], dpi, s).start()
            return 0

        lax.fori_loop(1, n_sh, body, 0)
        update(gb[k, f * ng + g, me], me)
        pltpu.make_async_copy(pan.at[k, me], panels.at[m, a, b, me, r, :], own_sem.at[k]).start()
        for i, (src, dst) in enumerate(((vp, o_p), (v1, o_1), (v2, o_2))):
            pltpu.make_async_copy(src.at[k], dst.at[m, r, :], out_sem.at[i, k]).start()

    def five(k, j, came=False):
        m, r = geometry(k)
        nf, ng, f, g, flat = dims(k)
        block = panels.at[m, a, b, :, r, :]
        return remote(block, block, s5s.at[k, j - 1], s5r.at[k, j - 1], flat((f + j) % nf, g), me)

    def stage4(k):
        m, r = geometry(k)
        nf = dims(k)[0]
        some = panels.at[m, a, b, pl.ds(0, n_sh - 1), r, :]
        pltpu.make_async_copy(some, some, s4r.at[k]).wait()
        pltpu.make_async_copy(pan.at[k, me], panels.at[m, a, b, me, r, :], own_sem.at[k]).wait()
        for j in range(1, nf):
            five(k, j).start()

    def six(k, j):
        m, r = geometry(k)
        nf, ng, f, g, flat = dims(k)
        block = panels.at[m, :, b, :, r, :] if k % 2 == 0 else panels.at[m, a, :, :, r, :]
        return remote(block, block, s6s.at[k, j - 1], s6r.at[k, j - 1], flat(f, (g + j) % ng), me)

    def stage5(k):
        nf, ng = dims(k)[:2]
        for j in range(1, nf):
            five(k, j).wait_recv()
        for j in range(1, ng):
            six(k, j).start()

    for k in range(chunks):
        load(k)

    barrier = pltpu.get_barrier_semaphore()
    for j in range(1, na):
        pl.semaphore_signal(barrier, inc=1, device_id=(((a + j) % na) * nb + b, me), device_id_type=MESH)
    for j in range(1, nb):
        pl.semaphore_signal(barrier, inc=1, device_id=(a * nb + (b + j) % nb, me), device_id_type=MESH)
    for j in range(1, n_sh):
        pl.semaphore_signal(barrier, inc=1, device_id=(dpi, (me + j) % n_sh), device_id_type=MESH)
    pl.semaphore_wait(barrier, na - 1 + nb - 1 + n_sh - 1)

    stages = (stage0, stage1, stage2, stage3, stage4, stage5)
    for t in range(chunks + LAGS[-1]):
        for n in (0, 5, 4, 3, 2, 1):
            k = t - LAGS[n]
            if 0 <= k < chunks:
                stages[n](k)

    for k in range(chunks):
        m, r = geometry(k)
        nf, ng = dims(k)[:2]
        for j in range(1, nf):
            one(k, j).wait_send()
            five(k, j).wait_send()
        for j in range(1, ng):
            two(k, j).wait_send()
            six(k, j).wait_send()
            six(k, j).wait_recv()
        some = r3.at[k]
        pltpu.make_async_copy(some, some, s3s.at[k]).wait()
        some = pan.at[k, pl.ds(0, n_sh - 1)]
        pltpu.make_async_copy(some, some, s4s.at[k]).wait()
        for i, (src, dst) in enumerate(((vp, o_p), (v1, o_1), (v2, o_2))):
            pltpu.make_async_copy(src.at[k], dst.at[m, r, :], out_sem.at[i, k]).wait()


def body(grads, params, moment_one, moment_two, relation_ids, rates, step_count):
    n_dp = lax.axis_size("dp")
    n_sh = lax.axis_size("shard")
    relations = grads.shape[1]
    mats = relations * 2
    pc = grads.shape[-1]
    width = pc * n_sh
    owned = params.shape[2]
    nb = 2 if n_dp % 2 == 0 else 1
    na = n_dp // nb
    rows = min(ROWS, owned)
    splits = owned // rows
    chunks = mats * splits
    onehot = (relation_ids[:, None] == jnp.arange(rates.shape[0], dtype=jnp.int32)[None, :]).astype(
        jnp.float32
    )
    learn = jnp.sum(onehot * rates[None, :], axis=1)
    steps = step_count[0].astype(jnp.float32)
    fix_one = 1.0 - jnp.power(jnp.float32(0.9), steps)
    fix_two = 1.0 - jnp.power(jnp.float32(0.95), steps)
    scal = jnp.concatenate([jnp.stack([1.0 / fix_one, 1.0 / fix_two]), learn])
    pieces = grads.reshape(mats, na, nb, n_sh, owned, pc)
    flat = [x.reshape(mats, owned, width) for x in (params, moment_one, moment_two)]
    state = jax.ShapeDtypeStruct((mats, owned, width), jnp.float32)
    first = n_dp - min(na, nb)
    second = max(na, nb) - 1
    hand = pl.BlockSpec(memory_space=pl.ANY)
    dma = pltpu.SemaphoreType.DMA
    most = second
    out = pl.pallas_call(
        functools.partial(kernel, (na, nb, n_sh, mats, relations, rows, splits, pc)),
        out_shape=(state, state, state,
                   jax.ShapeDtypeStruct((mats, na, nb, n_sh, owned, pc), jnp.bfloat16)),
        in_specs=[pl.BlockSpec(memory_space=pltpu.SMEM)] + [hand] * 4,
        out_specs=(hand,) * 4,
        scratch_shapes=[
            pltpu.VMEM((chunks, n_dp, n_sh, rows, pc), jnp.float32),
            pltpu.VMEM((chunks, rows, width), jnp.float32),
            pltpu.VMEM((chunks, rows, width), jnp.float32),
            pltpu.VMEM((chunks, rows, width), jnp.float32),
            pltpu.VMEM((chunks, first, n_sh, rows, pc), jnp.int16),
            pltpu.VMEM((chunks, first, n_sh, rows, pc), jnp.int16),
            pltpu.VMEM((chunks, second, n_sh, rows, pc), jnp.int16),
            pltpu.VMEM((chunks, second, n_sh, rows, pc), jnp.int16),
            pltpu.VMEM((chunks, n_sh - 1, rows, pc), jnp.float32),
            pltpu.VMEM((chunks, n_sh, rows, pc), jnp.bfloat16),
            dma((chunks,)),
            dma((3, chunks)),
            dma((3, chunks)),
            dma((chunks,)),
            dma((chunks, most)), dma((chunks, most)),
            dma((chunks, most)), dma((chunks, most)),
            dma((chunks,)), dma((chunks,)),
            dma((chunks,)), dma((chunks,)),
            dma((chunks, most)), dma((chunks, most)),
            dma((chunks, most)), dma((chunks, most)),
        ],
        compiler_params=pltpu.CompilerParams(
            collective_id=0, has_side_effects=True, vmem_limit_bytes=56 * 1024 * 1024),
        cost_estimate=pl.CostEstimate(flops=50 * mats * owned * width, bytes_accessed=56 * mats * owned * width // 1,
                                      transcendentals=0),
    )(scal, pieces, *flat)
    new_params, new_one, new_two = (x.reshape(params.shape) for x in out[:3])
    panels = out[3].reshape(relations, 2, owned * n_sh * n_dp, pc)
    return (new_params, new_one, new_two, panels)


def solution(mesh):
    in_specs = (
        P("dp", None, None, None, "shard"),
        P(None, None, ("dp", "shard"), None),
        P(None, None, ("dp", "shard"), None),
        P(None, None, ("dp", "shard"), None),
        P(),
        P(),
        P(),
    )
    out_specs = (
        P(None, None, ("dp", "shard"), None),
        P(None, None, ("dp", "shard"), None),
        P(None, None, ("dp", "shard"), None),
        P(None, None, None, "shard"),
    )
    return jax.shard_map(body, mesh=mesh, in_specs=in_specs, out_specs=out_specs, check_vma=False)
```

```python
import functools
import math

import jax
import jax.numpy as jnp
from jax import lax
from jax.experimental import pallas as pl
from jax.experimental.pallas import tpu as pltpu
from jax.sharding import PartitionSpec as P

LIMIT = 6.0
TOP = 32700.0
SOFT = 0.61
MESH = pl.DeviceIdType.MESH
LAGS = (0, 2, 4, 6, 8, 10)
ROWS = 16


def encode(x, limit):
    soft = SOFT * math.sqrt(limit)
    scale = TOP * math.sqrt(limit**2 + soft**2) / limit
    bent = x * lax.rsqrt(x * x + soft**2) * scale
    return jnp.round(bent).astype(jnp.int32).astype(jnp.int16)


def decode(code, limit):
    soft = SOFT * math.sqrt(limit)
    scale = TOP * math.sqrt(limit**2 + soft**2) / limit
    bent = code.astype(jnp.int32).astype(jnp.float32) * (1.0 / scale)
    return bent * lax.rsqrt(1.0 - bent * bent) * soft


def kernel(sizes, scal, grads, params, mone, mtwo, o_p, o_1, o_2, panels,
           gb, vp, v1, v2, c1, r1, c2, r2, c3, r3, pan,
           g_sem, in_sem, out_sem, own_sem, s1s, s1r, s2s, s2r, s3s, s3r, s4s, s4r, s5s, s5r, s6s, s6r):
    na, nb, n_sh, mats, relations, rows, splits, pc = sizes
    n_dp = na * nb
    chunks = mats * splits
    dpi = lax.axis_index("dp")
    me = lax.axis_index("shard")
    a, b = dpi // nb, dpi % nb

    def geometry(k):
        m, c = k // splits, k % splits
        return m, pl.ds(c * rows, rows)

    def dims(k):
        if k % 2 == 0:
            return na, nb, a, b, lambda f, g: f * nb + g
        return nb, na, b, a, lambda f, g: g * nb + f

    def load(k):
        m, r = geometry(k)
        nf, ng = dims(k)[:2]
        for f in range(nf):
            if k % 2 == 0:
                src = grads.at[m, f, :, :, r, :]
            else:
                src = grads.at[m, :, f, :, r, :]
            pltpu.make_async_copy(src, gb.at[k, pl.ds(f * ng, ng)], g_sem.at[k]).start()
        for i, (src, dst) in enumerate(((params, vp), (mone, v1), (mtwo, v2))):
            pltpu.make_async_copy(src.at[m, r, :], dst.at[k], in_sem.at[i, k]).start()

    def remote(src, dst, ss, rs, dp, sh):
        return pltpu.make_async_remote_copy(
            src_ref=src, dst_ref=dst, send_sem=ss, recv_sem=rs,
            device_id=(dp, sh), device_id_type=MESH)

    def one(k, j):
        nf, ng, f, g, flat = dims(k)
        part = pl.ds((j - 1) * ng, ng)
        return remote(c1.at[k, part], r1.at[k, part], s1s.at[k, j - 1], s1r.at[k, j - 1],
                      flat((f + j) % nf, g), me)

    def two(k, j):
        nf, ng, f, g, flat = dims(k)
        return remote(c2.at[k, j - 1], r2.at[k, j - 1], s2s.at[k, j - 1], s2r.at[k, j - 1],
                      flat(f, (g + j) % ng), me)

    def stage0(k):
        nf, ng, f, g, flat = dims(k)
        pltpu.make_async_copy(gb.at[k], gb.at[k], g_sem.at[k]).wait()
        for j in range(1, nf):
            to = (f + j) % nf

            def body(i, _):
                for h in range(ng):
                    c1[k, (j - 1) * ng + h, i] = encode(gb[k, to * ng + h, i], LIMIT)
                return 0

            lax.fori_loop(0, n_sh, body, 0)
            one(k, j).start()

    def stage1(k):
        nf, ng, f, g, flat = dims(k)
        for j in range(1, nf):
            one(k, j).wait_recv()

        def total(h, i):
            value = gb[k, f * ng + h, i]
            for j in range(1, nf):
                value = value + decode(r1[k, (j - 1) * ng + h, i], LIMIT)
            return value

        for j in range(1, ng):
            to = (g + j) % ng

            def body(i, _):
                c2[k, j - 1, i] = encode(total(to, i), LIMIT * nf)
                return 0

            lax.fori_loop(0, n_sh, body, 0)
            two(k, j).start()

        def own(i, _):
            gb[k, f * ng + g, i] = total(g, i)
            return 0

        lax.fori_loop(0, n_sh, own, 0)

    def stage2(k):
        nf, ng, f, g, flat = dims(k)
        for j in range(1, ng):
            two(k, j).wait_recv()

        def body(i, _):
            value = gb[k, f * ng + g, i]
            for j in range(1, ng):
                value = value + decode(r2[k, j - 1, i], LIMIT * nf)
            gb[k, f * ng + g, i] = value
            c3[k, i] = encode(value, LIMIT * n_dp)
            return 0

        lax.fori_loop(0, n_sh, body, 0)

        def send(j, _):
            to = (me + j) % n_sh
            remote(c3.at[k, to], r3.at[k, j - 1], s3s.at[k], s3r.at[k], dpi, to).start()
            return 0

        lax.fori_loop(1, n_sh, send, 0)

    def stage3(k):
        m, r = geometry(k)
        nf, ng, f, g, flat = dims(k)
        some = r3.at[k]
        pltpu.make_async_copy(some, some, s3r.at[k]).wait()
        for i, dst in enumerate((vp, v1, v2)):
            pltpu.make_async_copy(dst.at[k], dst.at[k], in_sem.at[i, k]).wait()
        rel = m // (mats // relations)
        learn = scal[2 + rel]
        inv_one, inv_two = scal[0], scal[1]

        def update(total, s):
            cols = pl.ds(pl.multiple_of(s * pc, 128), pc)
            gradient = total * (1.0 / n_dp)
            p = vp[k, :, cols]
            new_one = 0.9 * v1[k, :, cols] + 0.1 * gradient
            new_two = 0.95 * v2[k, :, cols] + 0.05 * gradient * gradient
            step = (new_one * inv_one) / (jnp.sqrt(new_two * inv_two) + 1e-08) + 0.1 * p
            new_p = p - learn * step
            vp[k, :, cols] = new_p
            v1[k, :, cols] = new_one
            v2[k, :, cols] = new_two
            pan[k, s] = new_p.astype(jnp.bfloat16)

        def body(j, _):
            s = (me + n_sh - j) % n_sh
            update(decode(r3[k, j - 1], LIMIT * n_dp), s)
            remote(pan.at[k, s], panels.at[m, a, b, me, r, :], s4s.at[k], s4r.at[k], dpi, s).start()
            return 0

        lax.fori_loop(1, n_sh, body, 0)
        update(gb[k, f * ng + g, me], me)
        pltpu.make_async_copy(pan.at[k, me], panels.at[m, a, b, me, r, :], own_sem.at[k]).start()
        for i, (src, dst) in enumerate(((vp, o_p), (v1, o_1), (v2, o_2))):
            pltpu.make_async_copy(src.at[k], dst.at[m, r, :], out_sem.at[i, k]).start()

    def five(k, j, came=False):
        m, r = geometry(k)
        nf, ng, f, g, flat = dims(k)
        block = panels.at[m, a, b, :, r, :]
        return remote(block, block, s5s.at[k, j - 1], s5r.at[k, j - 1], flat((f + j) % nf, g), me)

    def stage4(k):
        m, r = geometry(k)
        nf = dims(k)[0]
        some = panels.at[m, a, b, pl.ds(0, n_sh - 1), r, :]
        pltpu.make_async_copy(some, some, s4r.at[k]).wait()
        pltpu.make_async_copy(pan.at[k, me], panels.at[m, a, b, me, r, :], own_sem.at[k]).wait()
        for j in range(1, nf):
            five(k, j).start()

    def six(k, j):
        m, r = geometry(k)
        nf, ng, f, g, flat = dims(k)
        block = panels.at[m, :, b, :, r, :] if k % 2 == 0 else panels.at[m, a, :, :, r, :]
        return remote(block, block, s6s.at[k, j - 1], s6r.at[k, j - 1], flat(f, (g + j) % ng), me)

    def stage5(k):
        nf, ng = dims(k)[:2]
        for j in range(1, nf):
            five(k, j).wait_recv()
        for j in range(1, ng):
            six(k, j).start()

    for k in range(chunks):
        load(k)

    barrier = pltpu.get_barrier_semaphore()
    for j in range(1, na):
        pl.semaphore_signal(barrier, inc=1, device_id=(((a + j) % na) * nb + b, me), device_id_type=MESH)
    for j in range(1, nb):
        pl.semaphore_signal(barrier, inc=1, device_id=(a * nb + (b + j) % nb, me), device_id_type=MESH)
    for j in range(1, n_sh):
        pl.semaphore_signal(barrier, inc=1, device_id=(dpi, (me + j) % n_sh), device_id_type=MESH)
    pl.semaphore_wait(barrier, na - 1 + nb - 1 + n_sh - 1)

    stages = (stage0, stage1, stage2, stage3, stage4, stage5)
    for t in range(chunks + LAGS[-1]):
        for n in (0, 5, 4, 3, 2, 1):
            k = t - LAGS[n]
            if 0 <= k < chunks:
                stages[n](k)

    for k in range(chunks):
        m, r = geometry(k)
        nf, ng = dims(k)[:2]
        for j in range(1, nf):
            one(k, j).wait_send()
            five(k, j).wait_send()
        for j in range(1, ng):
            two(k, j).wait_send()
            six(k, j).wait_send()
            six(k, j).wait_recv()
        some = r3.at[k]
        pltpu.make_async_copy(some, some, s3s.at[k]).wait()
        some = pan.at[k, pl.ds(0, n_sh - 1)]
        pltpu.make_async_copy(some, some, s4s.at[k]).wait()
        for i, (src, dst) in enumerate(((vp, o_p), (v1, o_1), (v2, o_2))):
            pltpu.make_async_copy(src.at[k], dst.at[m, r, :], out_sem.at[i, k]).wait()


def body(grads, params, moment_one, moment_two, relation_ids, rates, step_count):
    n_dp = lax.axis_size("dp")
    n_sh = lax.axis_size("shard")
    relations = grads.shape[1]
    mats = relations * 2
    pc = grads.shape[-1]
    width = pc * n_sh
    owned = params.shape[2]
    nb = 2 if n_dp % 2 == 0 else 1
    na = n_dp // nb
    rows = min(ROWS, owned)
    splits = owned // rows
    chunks = mats * splits
    onehot = (relation_ids[:, None] == jnp.arange(rates.shape[0], dtype=jnp.int32)[None, :]).astype(
        jnp.float32
    )
    learn = jnp.sum(onehot * rates[None, :], axis=1)
    steps = step_count[0].astype(jnp.float32)
    fix_one = 1.0 - jnp.power(jnp.float32(0.9), steps)
    fix_two = 1.0 - jnp.power(jnp.float32(0.95), steps)
    scal = jnp.concatenate([jnp.stack([1.0 / fix_one, 1.0 / fix_two]), learn])
    pieces = grads.reshape(mats, na, nb, n_sh, owned, pc)
    flat = [x.reshape(mats, owned, width) for x in (params, moment_one, moment_two)]
    state = jax.ShapeDtypeStruct((mats, owned, width), jnp.float32)
    first = n_dp - min(na, nb)
    second = max(na, nb) - 1
    hand = pl.BlockSpec(memory_space=pl.ANY)
    dma = pltpu.SemaphoreType.DMA
    most = second
    out = pl.pallas_call(
        functools.partial(kernel, (na, nb, n_sh, mats, relations, rows, splits, pc)),
        out_shape=(state, state, state,
                   jax.ShapeDtypeStruct((mats, na, nb, n_sh, owned, pc), jnp.bfloat16)),
        in_specs=[pl.BlockSpec(memory_space=pltpu.SMEM)] + [hand] * 4,
        out_specs=(hand,) * 4,
        scratch_shapes=[
            pltpu.VMEM((chunks, n_dp, n_sh, rows, pc), jnp.float32),
            pltpu.VMEM((chunks, rows, width), jnp.float32),
            pltpu.VMEM((chunks, rows, width), jnp.float32),
            pltpu.VMEM((chunks, rows, width), jnp.float32),
            pltpu.VMEM((chunks, first, n_sh, rows, pc), jnp.int16),
            pltpu.VMEM((chunks, first, n_sh, rows, pc), jnp.int16),
            pltpu.VMEM((chunks, second, n_sh, rows, pc), jnp.int16),
            pltpu.VMEM((chunks, second, n_sh, rows, pc), jnp.int16),
            pltpu.VMEM((chunks, n_sh, rows, pc), jnp.int16),
            pltpu.VMEM((chunks, n_sh - 1, rows, pc), jnp.int16),
            pltpu.VMEM((chunks, n_sh, rows, pc), jnp.bfloat16),
            dma((chunks,)),
            dma((3, chunks)),
            dma((3, chunks)),
            dma((chunks,)),
            dma((chunks, most)), dma((chunks, most)),
            dma((chunks, most)), dma((chunks, most)),
            dma((chunks,)), dma((chunks,)),
            dma((chunks,)), dma((chunks,)),
            dma((chunks, most)), dma((chunks, most)),
            dma((chunks, most)), dma((chunks, most)),
        ],
        compiler_params=pltpu.CompilerParams(
            collective_id=0, has_side_effects=True, vmem_limit_bytes=56 * 1024 * 1024),
        cost_estimate=pl.CostEstimate(flops=50 * mats * owned * width, bytes_accessed=56 * mats * owned * width // 1,
                                      transcendentals=0),
    )(scal, pieces, *flat)
    new_params, new_one, new_two = (x.reshape(params.shape) for x in out[:3])
    panels = out[3].reshape(relations, 2, owned * n_sh * n_dp, pc)
    return (new_params, new_one, new_two, panels)


def solution(mesh):
    in_specs = (
        P("dp", None, None, None, "shard"),
        P(None, None, ("dp", "shard"), None),
        P(None, None, ("dp", "shard"), None),
        P(None, None, ("dp", "shard"), None),
        P(),
        P(),
        P(),
    )
    out_specs = (
        P(None, None, ("dp", "shard"), None),
        P(None, None, ("dp", "shard"), None),
        P(None, None, ("dp", "shard"), None),
        P(None, None, None, "shard"),
    )
    return jax.shard_map(body, mesh=mesh, in_specs=in_specs, out_specs=out_specs, check_vma=False)
```

```python
import functools
import math

import jax
import jax.numpy as jnp
from jax import lax
from jax.experimental import pallas as pl
from jax.experimental.pallas import tpu as pltpu
from jax.sharding import PartitionSpec as P

LIMIT = 6.0
TOP = 32700.0
SOFT = 0.61
MESH = pl.DeviceIdType.MESH
LAGS = (0, 2, 4, 6, 8, 10)
ROWS = 16


def encode(x, limit):
    soft = SOFT * math.sqrt(limit)
    scale = TOP * math.sqrt(limit**2 + soft**2) / limit
    bent = x * lax.rsqrt(x * x + soft**2) * scale
    return jnp.round(bent).astype(jnp.int32).astype(jnp.int16)


def decode(code, limit):
    soft = SOFT * math.sqrt(limit)
    scale = TOP * math.sqrt(limit**2 + soft**2) / limit
    bent = code.astype(jnp.int32).astype(jnp.float32) * (1.0 / scale)
    return bent * lax.rsqrt(1.0 - bent * bent) * soft


def kernel(sizes, ids, rates, count, grads, params, mone, mtwo, o_p, o_1, o_2, panels,
           gb, vp, v1, v2, c1, r1, c2, r2, c3, r3, pan,
           g_sem, in_sem, out_sem, own_sem, s1s, s1r, s2s, s2r, s3s, s3r, s4s, s4r, s5s, s5r, s6s, s6r):
    na, nb, n_sh, mats, relations, rows, splits, pc = sizes
    n_dp = na * nb
    chunks = mats * splits
    dpi = lax.axis_index("dp")
    me = lax.axis_index("shard")
    a, b = dpi // nb, dpi % nb

    def geometry(k):
        m, c = k // splits, k % splits
        return m, pl.ds(c * rows, rows)

    def dims(k):
        if k % 2 == 0:
            return na, nb, a, b, lambda f, g: f * nb + g
        return nb, na, b, a, lambda f, g: g * nb + f

    def load(k):
        m, r = geometry(k)
        nf, ng = dims(k)[:2]
        for f in range(nf):
            if k % 2 == 0:
                src = grads.at[m, f, :, :, r, :]
            else:
                src = grads.at[m, :, f, :, r, :]
            pltpu.make_async_copy(src, gb.at[k, pl.ds(f * ng, ng)], g_sem.at[k]).start()
        for i, (src, dst) in enumerate(((params, vp), (mone, v1), (mtwo, v2))):
            pltpu.make_async_copy(src.at[m, r, :], dst.at[k], in_sem.at[i, k]).start()

    def remote(src, dst, ss, rs, dp, sh):
        return pltpu.make_async_remote_copy(
            src_ref=src, dst_ref=dst, send_sem=ss, recv_sem=rs,
            device_id=(dp, sh), device_id_type=MESH)

    def one(k, j):
        nf, ng, f, g, flat = dims(k)
        part = pl.ds((j - 1) * ng, ng)
        return remote(c1.at[k, part], r1.at[k, part], s1s.at[k, j - 1], s1r.at[k, j - 1],
                      flat((f + j) % nf, g), me)

    def two(k, j):
        nf, ng, f, g, flat = dims(k)
        return remote(c2.at[k, j - 1], r2.at[k, j - 1], s2s.at[k, j - 1], s2r.at[k, j - 1],
                      flat(f, (g + j) % ng), me)

    def stage0(k):
        nf, ng, f, g, flat = dims(k)
        pltpu.make_async_copy(gb.at[k], gb.at[k], g_sem.at[k]).wait()
        for j in range(1, nf):
            to = (f + j) % nf

            def body(i, _):
                for h in range(ng):
                    c1[k, (j - 1) * ng + h, i] = encode(gb[k, to * ng + h, i], LIMIT)
                return 0

            lax.fori_loop(0, n_sh, body, 0)
            one(k, j).start()

    def stage1(k):
        nf, ng, f, g, flat = dims(k)
        for j in range(1, nf):
            one(k, j).wait_recv()

        def total(h, i):
            value = gb[k, f * ng + h, i]
            for j in range(1, nf):
                value = value + decode(r1[k, (j - 1) * ng + h, i], LIMIT)
            return value

        for j in range(1, ng):
            to = (g + j) % ng

            def body(i, _):
                c2[k, j - 1, i] = encode(total(to, i), LIMIT * nf)
                return 0

            lax.fori_loop(0, n_sh, body, 0)
            two(k, j).start()

        def own(i, _):
            gb[k, f * ng + g, i] = total(g, i)
            return 0

        lax.fori_loop(0, n_sh, own, 0)

    def stage2(k):
        nf, ng, f, g, flat = dims(k)
        for j in range(1, ng):
            two(k, j).wait_recv()

        def body(i, _):
            value = gb[k, f * ng + g, i]
            for j in range(1, ng):
                value = value + decode(r2[k, j - 1, i], LIMIT * nf)
            gb[k, f * ng + g, i] = value
            c3[k, i] = encode(value, LIMIT * n_dp)
            return 0

        lax.fori_loop(0, n_sh, body, 0)

        def send(j, _):
            to = (me + j) % n_sh
            remote(c3.at[k, to], r3.at[k, j - 1], s3s.at[k], s3r.at[k], dpi, to).start()
            return 0

        lax.fori_loop(1, n_sh, send, 0)

    def stage3(k):
        m, r = geometry(k)
        nf, ng, f, g, flat = dims(k)
        some = r3.at[k]
        pltpu.make_async_copy(some, some, s3r.at[k]).wait()
        for i, dst in enumerate((vp, v1, v2)):
            pltpu.make_async_copy(dst.at[k], dst.at[k], in_sem.at[i, k]).wait()
        rel = m // (mats // relations)
        learn = rates[ids[rel]]
        steps = jnp.full((1, pc), count[0].astype(jnp.float32))
        inv_one = 1.0 / (1.0 - jnp.exp(steps * math.log(0.9)))
        inv_two = 1.0 / (1.0 - jnp.exp(steps * math.log(0.95)))

        def update(total, s):
            cols = pl.ds(pl.multiple_of(s * pc, 128), pc)
            gradient = total * (1.0 / n_dp)
            p = vp[k, :, cols]
            new_one = 0.9 * v1[k, :, cols] + 0.1 * gradient
            new_two = 0.95 * v2[k, :, cols] + 0.05 * gradient * gradient
            step = (new_one * inv_one) / (jnp.sqrt(new_two * inv_two) + 1e-08) + 0.1 * p
            new_p = p - learn * step
            vp[k, :, cols] = new_p
            v1[k, :, cols] = new_one
            v2[k, :, cols] = new_two
            pan[k, s] = new_p.astype(jnp.bfloat16)

        def body(j, _):
            s = (me + n_sh - j) % n_sh
            update(decode(r3[k, j - 1], LIMIT * n_dp), s)
            remote(pan.at[k, s], panels.at[m, a, b, me, r, :], s4s.at[k], s4r.at[k], dpi, s).start()
            return 0

        lax.fori_loop(1, n_sh, body, 0)
        update(gb[k, f * ng + g, me], me)
        pltpu.make_async_copy(pan.at[k, me], panels.at[m, a, b, me, r, :], own_sem.at[k]).start()
        for i, (src, dst) in enumerate(((vp, o_p), (v1, o_1), (v2, o_2))):
            pltpu.make_async_copy(src.at[k], dst.at[m, r, :], out_sem.at[i, k]).start()

    def five(k, j, came=False):
        m, r = geometry(k)
        nf, ng, f, g, flat = dims(k)
        block = panels.at[m, a, b, :, r, :]
        return remote(block, block, s5s.at[k, j - 1], s5r.at[k, j - 1], flat((f + j) % nf, g), me)

    def stage4(k):
        m, r = geometry(k)
        nf = dims(k)[0]
        some = panels.at[m, a, b, pl.ds(0, n_sh - 1), r, :]
        pltpu.make_async_copy(some, some, s4r.at[k]).wait()
        pltpu.make_async_copy(pan.at[k, me], panels.at[m, a, b, me, r, :], own_sem.at[k]).wait()
        for j in range(1, nf):
            five(k, j).start()

    def six(k, j):
        m, r = geometry(k)
        nf, ng, f, g, flat = dims(k)
        block = panels.at[m, :, b, :, r, :] if k % 2 == 0 else panels.at[m, a, :, :, r, :]
        return remote(block, block, s6s.at[k, j - 1], s6r.at[k, j - 1], flat(f, (g + j) % ng), me)

    def stage5(k):
        nf, ng = dims(k)[:2]
        for j in range(1, nf):
            five(k, j).wait_recv()
        for j in range(1, ng):
            six(k, j).start()

    for k in range(chunks):
        load(k)

    barrier = pltpu.get_barrier_semaphore()
    for j in range(1, na):
        pl.semaphore_signal(barrier, inc=1, device_id=(((a + j) % na) * nb + b, me), device_id_type=MESH)
    for j in range(1, nb):
        pl.semaphore_signal(barrier, inc=1, device_id=(a * nb + (b + j) % nb, me), device_id_type=MESH)
    for j in range(1, n_sh):
        pl.semaphore_signal(barrier, inc=1, device_id=(dpi, (me + j) % n_sh), device_id_type=MESH)
    pl.semaphore_wait(barrier, na - 1 + nb - 1 + n_sh - 1)

    stages = (stage0, stage1, stage2, stage3, stage4, stage5)
    for t in range(chunks + LAGS[-1]):
        for n in (0, 5, 4, 3, 2, 1):
            k = t - LAGS[n]
            if 0 <= k < chunks:
                stages[n](k)

    for k in range(chunks):
        m, r = geometry(k)
        nf, ng = dims(k)[:2]
        for j in range(1, nf):
            one(k, j).wait_send()
            five(k, j).wait_send()
        for j in range(1, ng):
            two(k, j).wait_send()
            six(k, j).wait_send()
            six(k, j).wait_recv()
        some = r3.at[k]
        pltpu.make_async_copy(some, some, s3s.at[k]).wait()
        some = pan.at[k, pl.ds(0, n_sh - 1)]
        pltpu.make_async_copy(some, some, s4s.at[k]).wait()
        for i, (src, dst) in enumerate(((vp, o_p), (v1, o_1), (v2, o_2))):
            pltpu.make_async_copy(src.at[k], dst.at[m, r, :], out_sem.at[i, k]).wait()


def body(grads, params, moment_one, moment_two, relation_ids, rates, step_count):
    n_dp = lax.axis_size("dp")
    n_sh = lax.axis_size("shard")
    relations = grads.shape[1]
    mats = relations * 2
    pc = grads.shape[-1]
    width = pc * n_sh
    owned = params.shape[2]
    nb = 2 if n_dp % 2 == 0 else 1
    na = n_dp // nb
    rows = min(ROWS, owned)
    splits = owned // rows
    chunks = mats * splits
    pieces = grads.reshape(mats, na, nb, n_sh, owned, pc)
    flat = [x.reshape(mats, owned, width) for x in (params, moment_one, moment_two)]
    state = jax.ShapeDtypeStruct((mats, owned, width), jnp.float32)
    first = n_dp - min(na, nb)
    second = max(na, nb) - 1
    hand = pl.BlockSpec(memory_space=pl.ANY)
    dma = pltpu.SemaphoreType.DMA
    most = second
    out = pl.pallas_call(
        functools.partial(kernel, (na, nb, n_sh, mats, relations, rows, splits, pc)),
        out_shape=(state, state, state,
                   jax.ShapeDtypeStruct((mats, na, nb, n_sh, owned, pc), jnp.bfloat16)),
        in_specs=[pl.BlockSpec(memory_space=pltpu.SMEM)] * 3 + [hand] * 4,
        out_specs=(hand,) * 4,
        scratch_shapes=[
            pltpu.VMEM((chunks, n_dp, n_sh, rows, pc), jnp.float32),
            pltpu.VMEM((chunks, rows, width), jnp.float32),
            pltpu.VMEM((chunks, rows, width), jnp.float32),
            pltpu.VMEM((chunks, rows, width), jnp.float32),
            pltpu.VMEM((chunks, first, n_sh, rows, pc), jnp.int16),
            pltpu.VMEM((chunks, first, n_sh, rows, pc), jnp.int16),
            pltpu.VMEM((chunks, second, n_sh, rows, pc), jnp.int16),
            pltpu.VMEM((chunks, second, n_sh, rows, pc), jnp.int16),
            pltpu.VMEM((chunks, n_sh, rows, pc), jnp.int16),
            pltpu.VMEM((chunks, n_sh - 1, rows, pc), jnp.int16),
            pltpu.VMEM((chunks, n_sh, rows, pc), jnp.bfloat16),
            dma((chunks,)),
            dma((3, chunks)),
            dma((3, chunks)),
            dma((chunks,)),
            dma((chunks, most)), dma((chunks, most)),
            dma((chunks, most)), dma((chunks, most)),
            dma((chunks,)), dma((chunks,)),
            dma((chunks,)), dma((chunks,)),
            dma((chunks, most)), dma((chunks, most)),
            dma((chunks, most)), dma((chunks, most)),
        ],
        compiler_params=pltpu.CompilerParams(
            collective_id=0, has_side_effects=True, vmem_limit_bytes=56 * 1024 * 1024),
        cost_estimate=pl.CostEstimate(flops=50 * mats * owned * width, bytes_accessed=56 * mats * owned * width // 1,
                                      transcendentals=0),
    )(relation_ids, rates, step_count, pieces, *flat)
    new_params, new_one, new_two = (x.reshape(params.shape) for x in out[:3])
    panels = out[3].reshape(relations, 2, owned * n_sh * n_dp, pc)
    return (new_params, new_one, new_two, panels)


def solution(mesh):
    in_specs = (
        P("dp", None, None, None, "shard"),
        P(None, None, ("dp", "shard"), None),
        P(None, None, ("dp", "shard"), None),
        P(None, None, ("dp", "shard"), None),
        P(),
        P(),
        P(),
    )
    out_specs = (
        P(None, None, ("dp", "shard"), None),
        P(None, None, ("dp", "shard"), None),
        P(None, None, ("dp", "shard"), None),
        P(None, None, None, "shard"),
    )
    return jax.shard_map(body, mesh=mesh, in_specs=in_specs, out_specs=out_specs, check_vma=False)
```
